512 devices in a mesh: gx: 32 (over y, x_lo, core), gy: 16 (over x_hi, z).
Axes of the slice: x: 4 (x_hi: 2, x_lo: 2; x = x_hi * 2 + x_lo), y: 8, z: 8, core: 2. Of those that a mesh axis runs over, the one named last changes fastest.
Arguments:
- obstacles: int32 [4096, 4096], P('gx', 'gy'), may hold values 0 or 1
- load: float32 [4096, 4096], P('gx', 'gy'), may hold values from 0.25 to 4
- exit_rows: int32 [4, 4096], replicated, may hold values from 0 to 4095
- exit_cols: int32 [4, 4096], replicated, may hold values from 0 to 4095
Outputs:
- potential: float32 [4, 4096, 4096], P(None, 'gx', 'gy')
The draws below stay inside these ranges and needn't reach their ends.
All inputs are finite; a program needn't handle non-finite values. No bound on the sum of `obstacles` on one device may be relied on, other than what follows from the above.
Results may differ from the reference program's by a relative error of at most 0.0001.
Values sent between devices are 32-bit elements; how exact they have to be, the bound alone decides.
No kernel may reach another device: no remote copies, remote signals or barrier semaphores. Data moves between devices by JAX's collectives and lax.ppermute only.
A program may use at most 64 MiB of HBM per device.

```python
import jax
import jax.numpy as jnp

GOALS = 4
COARSEN = 4
SMOOTH = 4
CSWEEPS = 4
CYCLES = 2
NX = 4096
NY = 4096
EXITS = 4096


def draw_load(key, part):
    rough_part = jax.random.uniform(key, (NX, NY), jnp.float32, 0.25, 2.0)
    return rough_part


def touch_ends(values, own_key, smallest, largest):
    index_at = [jax.random.randint(jax.random.fold_in(own_key, axis), (), 0, length) for axis, length in enumerate(values.shape)]
    main_axis = values.shape.index(max(values.shape))
    beside = index_at[:main_axis] + [(index_at[main_axis] + 1) % values.shape[main_axis]] + index_at[main_axis + 1:]
    return values.at[tuple(index_at)].set(smallest).at[tuple(beside)].set(largest)


def setup_inputs(seed: int = 0) -> dict:
    key_of = jax.random.split(jax.random.key(seed), 5)
    return {
        "obstacles": touch_ends((jax.random.randint(key_of[0], (NX, NY), 0, 5) < 1).astype(jnp.int32), jax.random.fold_in(key_of[0], 1), 0, 1),
        "load": draw_load(jax.random.fold_in(key_of[4], 71), 0),
        "exit_rows": touch_ends(jax.random.randint(key_of[2], (GOALS, EXITS), 0, NX), jax.random.fold_in(key_of[2], 1), 0, NX - 1).astype(jnp.int32),
        "exit_cols": touch_ends(jax.random.randint(key_of[3], (GOALS, EXITS), 0, NY), jax.random.fold_in(key_of[3], 1), 0, NY - 1).astype(jnp.int32),
    }


SCREENING = 1e-4
EXIT_SINK = 4.0
COARSE_SHIFT = 0.01
DAMPING = 0.8
UPPER_BOUND = 12.5
LOWER_BOUND = 1.0


def cross_sum(field):
    padded = jnp.pad(field, ((0, 0), (1, 1), (1, 1)))
    return padded[:, 2:, 1:-1] + padded[:, :-2, 1:-1] + padded[:, 1:-1, 2:] + padded[:, 1:-1, :-2]


def chebyshev(start, residual, operate):
    center = 0.5 * (UPPER_BOUND + LOWER_BOUND)
    half_span = 0.5 * (UPPER_BOUND - LOWER_BOUND)
    sigma_ratio = center / half_span
    ratio_old = 1.0 / sigma_ratio
    update = residual / center
    result = start + update
    for sweep in range(SMOOTH - 1):
        residual = residual - operate(update)
        ratio_new = 1.0 / (2.0 * sigma_ratio - ratio_old)
        update = (ratio_new * ratio_old) * update + (2.0 * ratio_new / half_span) * residual
        result = result + update
        ratio_old = ratio_new
    return result


def restrict(residual):
    goals, height, width = residual.shape
    blocks = residual.reshape(goals, height // COARSEN, COARSEN, width // COARSEN, COARSEN)
    return blocks.mean(axis=(2, 4))


def coarse_solve(coarse_rhs):
    center_weight = 4.0 + COARSE_SHIFT
    estimate = DAMPING * coarse_rhs / center_weight
    for sweep in range(CSWEEPS - 1):
        estimate = estimate + DAMPING * (coarse_rhs - (center_weight * estimate - cross_sum(estimate))) / center_weight
    return estimate


def prolong(estimate, open_cells):
    expanded = jnp.repeat(jnp.repeat(estimate, COARSEN, axis=1), COARSEN, axis=2)
    return open_cells * expanded


def reference(obstacles, load, exit_rows, exit_cols):
    open_cells = (1 - obstacles).astype(jnp.float32)
    neighbours = cross_sum(open_cells[None])[0]
    goals = exit_rows.shape[0]
    flat_index = (exit_rows * NY + exit_cols).astype(jnp.int32)
    goal_index = jnp.broadcast_to(jnp.arange(goals, dtype=jnp.int32)[:, None], flat_index.shape)
    marks = jnp.zeros((goals, NX * NY), jnp.float32).at[goal_index, flat_index].add(1.0)
    exits = jnp.minimum(marks, 1.0).reshape(goals, NX, NY)
    diagonal = SCREENING + 4.0 * (1.0 - open_cells) + open_cells * neighbours + EXIT_SINK * open_cells * exits

    def operate(field):
        return diagonal * field - open_cells * cross_sum(open_cells * field)

    source = jnp.broadcast_to(open_cells * load, (goals, NX, NY))
    potential = chebyshev(jnp.zeros_like(source), source, operate)
    estimate = coarse_solve(restrict(source))
    for cycle in range(1, CYCLES):
        correction = prolong(estimate, open_cells)
        residual = source - operate(potential)
        shifted = residual - operate(correction)
        estimate_next = coarse_solve(restrict(residual))
        potential = chebyshev(potential + correction, shifted, operate)
        estimate = estimate_next
    return potential + prolong(estimate, open_cells)
```

```python
import functools

import jax
import jax.numpy as jnp
import numpy as np
from jax import lax
from jax.experimental import pallas as pl
from jax.experimental.pallas import tpu as pltpu
from jax.sharding import PartitionSpec as P

SCREENING = 0.0001
EXIT_SINK = 4.0
WEIGHT = 4.01
DAMPING = 0.8
CENTER = 6.75
HALF = 5.75

GOALS = 4
ROWS = 128
COLS = 256
HALO = 16
WIDE = ROWS + 2 * HALO
LANES = 384
PAD = 8
CROWS = WIDE // 4
CHUNK = 16
F32 = jnp.float32
BF16 = jnp.bfloat16

COEF = []
_q = CENTER / HALF
_p = 1.0 / _q
for _ in range(3):
    _n = 1.0 / (2.0 * _q - _p)
    COEF.append((_n * _p, 2.0 * _n / HALF))
    _p = _n


def split(x):
    high = x.astype(BF16)
    return high, (x - high.astype(F32)).astype(BF16)


def dot(a, b, dims=((1,), (0,))):
    return lax.dot_general(a, b, (dims, ((), ())), preferred_element_type=F32)


def iota(shape, dim):
    return lax.broadcasted_iota(jnp.int32, shape, dim)


def one_zero(condition):
    return jnp.where(condition, 1.0, 0.0).astype(F32)


def exits_kernel(rows_ref, cols_ref, out_ref):
    row0 = lax.axis_index("gx") * ROWS - HALO
    col0 = lax.axis_index("gy") * COLS
    step = 1024
    count = rows_ref.shape[1] // step
    row_at = iota((WIDE, step), 0)
    col_at = iota((COLS + 2 * HALO, step), 0)
    lane = iota((WIDE, 128), 1)

    def goal(g, carry):
        def part(k, total):
            at = pl.ds(pl.multiple_of(k * step, step), step)
            r = rows_ref[pl.ds(g, 1), at] - row0
            c = cols_ref[pl.ds(g, 1), at] - col0
            near = (c >= -HALO) & (c < COLS + HALO)
            c = jnp.where(c < 0, c + COLS + HALO, jnp.where(c >= COLS, c + HALO, c))
            c = jnp.where(near, c, -1)
            left = one_zero(row_at == r).astype(BF16)
            right = one_zero(col_at == c).astype(BF16)
            return total + dot(left, right, ((1,), (1,)))

        total = lax.fori_loop(0, count, part, jnp.zeros((WIDE, COLS + 2 * HALO), F32))
        sink = jnp.minimum(total, 1.0) * EXIT_SINK
        out_ref[g, :, 0:COLS] = sink[:, :COLS]
        tail = jnp.concatenate([sink[:, COLS:], jnp.zeros((WIDE, 128 - 2 * HALO), F32)], axis=1)
        out_ref[g, :, COLS:LANES] = pltpu.roll(tail, 128 - HALO, 1)
        return carry

    lax.fori_loop(0, GOALS, goal, 0)


def exits_of(rows, cols):
    return pl.pallas_call(
        exits_kernel,
        out_shape=jax.ShapeDtypeStruct((GOALS, WIDE, LANES), F32),
        in_specs=[pl.BlockSpec(memory_space=pltpu.VMEM)] * 2,
        out_specs=pl.BlockSpec(memory_space=pltpu.VMEM),
        compiler_params=pltpu.CompilerParams(vmem_limit_bytes=32 * 2**20),
        cost_estimate=pl.CostEstimate(flops=2 * 4 * 4096 * 160 * 288, bytes_accessed=2**20, transcendentals=0),
    )(rows, cols)


def pack_kernel(src_ref, top_ref, bottom_ref, left_ref, right_ref):
    def tile(q, lo):
        if q < HALO // 8:
            return top_ref[8 * q : 8 * q + 8, lo : lo + 128]
        if q >= (HALO + ROWS) // 8:
            at = 8 * q - HALO - ROWS
            return bottom_ref[at : at + 8, lo : lo + 128]
        at = 8 * q - HALO
        return src_ref[at : at + 8, lo : lo + 128]

    lane = iota((8, 128), 1)
    for b in range(LANES // 128):
        left = jnp.zeros((8, 128), F32)
        right = jnp.zeros((8, 128), F32)
        for m in range(8):
            q = 8 * b + m
            if q >= WIDE // 8:
                break
            here = (lane >= HALO * m) & (lane < HALO * (m + 1))
            left = jnp.where(here, pltpu.roll(tile(q, 0), HALO * m, 1), left)
            right = jnp.where(here, pltpu.roll(tile(q, COLS - 128), (HALO * m + HALO) % 128, 1), right)
        left_ref[:, 128 * b : 128 * b + 128] = left
        right_ref[:, 128 * b : 128 * b + 128] = right


def pack(src, top, bottom):
    return pl.pallas_call(
        pack_kernel,
        out_shape=[jax.ShapeDtypeStruct((8, LANES), F32)] * 2,
        in_specs=[pl.BlockSpec(memory_space=pltpu.VMEM)] * 3,
        out_specs=[pl.BlockSpec(memory_space=pltpu.VMEM)] * 2,
    )(src, top, bottom)


def main_kernel(
    src_ref, top_ref, bottom_ref, from_left_ref, from_right_ref, exits_ref, out_ref,
    s_ref, o_ref, diag_ref, r1_ref, corr_ref, shift_ref, da_ref, db_ref, r_ref, x_ref, pool_ref, grow_ref,
):
    gx, gy = lax.axis_index("gx"), lax.axis_index("gy")
    zero = jnp.zeros((PAD, LANES), F32)
    for ref in (s_ref, o_ref, corr_ref, da_ref, db_ref):
        ref[0:PAD, :] = zero
        ref[PAD + WIDE : 2 * PAD + WIDE, :] = zero

    s_ref[PAD : PAD + HALO, 0:COLS] = top_ref[...]
    s_ref[PAD + HALO : PAD + HALO + ROWS, 0:COLS] = src_ref[...]
    s_ref[PAD + HALO + ROWS : PAD + WIDE, 0:COLS] = bottom_ref[...]
    lane = iota((8, 128), 1)
    for q in range(WIDE // 8):
        b, m = divmod(q, 8)
        at = slice(128 * b, 128 * b + 128)
        ahead = pltpu.roll(from_right_ref[:, at], (128 - HALO * m) % 128, 1)
        behind = pltpu.roll(from_left_ref[:, at], (128 - HALO - HALO * m) % 128, 1)
        both = jnp.where(lane < HALO, ahead, jnp.where(lane >= 128 - HALO, behind, 0.0))
        s_ref[PAD + 8 * q : PAD + 8 * q + 8, COLS:LANES] = both

    chunks = range(0, WIDE, CHUNK)

    def pad_at(i, shift=0):
        return slice(PAD + i + shift, PAD + i + shift + CHUNK)

    def at(i):
        return slice(i, i + CHUNK)

    def cross(ref, i, mid):
        ends = ref[pad_at(i, 1), :] + ref[pad_at(i, -1), :]
        return ends + (pltpu.roll(mid, LANES - 1, 1) + pltpu.roll(mid, 1, 1))

    for i in chunks:
        o_ref[pad_at(i), :] = one_zero(s_ref[pad_at(i), :] > 0.0)
    for i in chunks:
        o, s = o_ref[pad_at(i), :], s_ref[pad_at(i), :]
        diag = SCREENING + 4.0 * (1.0 - o) + o * cross(o_ref, i, o)
        diag_ref[at(i), :] = diag
        d = s * (1.0 / CENTER)
        r1_ref[at(i), :] = s - diag * d + o * (cross(s_ref, i, s) * (1.0 / CENTER))

    fine_col, coarse_col = iota((LANES, 128), 0), iota((LANES, 128), 1)
    fine_col = jnp.where(fine_col >= 320, fine_col - LANES, fine_col)
    coarse_col = jnp.where(coarse_col >= 96, coarse_col - 128, coarse_col)
    gather_cols = jnp.where((fine_col >> 2) == coarse_col, 0.25, 0.0).astype(BF16)
    fine_row, coarse_row = iota((CROWS, WIDE), 1), iota((CROWS, WIDE), 0)
    gather_rows = jnp.where((fine_row >> 2) == coarse_row, 0.25, 0.0).astype(BF16)
    gather_rows = jnp.concatenate([gather_rows, gather_rows], axis=1)
    spread_c, spread_f = iota((256, LANES), 0) & 127, iota((256, LANES), 1)
    spread_c = jnp.where(spread_c >= 96, spread_c - 128, spread_c)
    spread_f = jnp.where(spread_f >= 320, spread_f - LANES, spread_f)
    spread_cols = one_zero(spread_c == (spread_f >> 2)).astype(BF16)
    sr_f, sr_c = iota((WIDE, 2 * CROWS), 0), iota((WIDE, 2 * CROWS), 1)
    sr_c = jnp.where(sr_c >= CROWS, sr_c - CROWS, sr_c)
    spread_rows = one_zero((sr_f >> 2) == sr_c).astype(BF16)

    def restrict(field):
        high, low = split(field)
        part = dot(high, gather_cols) + dot(low, gather_cols)
        high, low = split(part)
        return dot(gather_rows, jnp.concatenate([high, low], axis=0))

    def prolong_cols(e):
        high, low = split(e)
        return dot(jnp.concatenate([high, low], axis=1), spread_cols)

    def prolong_rows(e, spread):
        high, low = split(e)
        return dot(spread, jnp.concatenate([high, low], axis=0))

    def coarse(f):
        n = f.shape[0]
        row = gx * (ROWS // 4) + (lax.rem(iota((n, 128), 0), CROWS) - HALO // 4)
        col = iota((n, 128), 1)
        col = gy * (COLS // 4) + jnp.where(col >= 96, col - 128, col)
        inside = (row >= 0) & (row < 32 * (ROWS // 4)) & (col >= 0) & (col < 16 * (COLS // 4))
        mask = one_zero(inside)
        f = f * (DAMPING / WEIGHT)
        e = f * mask
        for _ in range(3):
            cr = (pltpu.roll(e, n - 1, 0) + pltpu.roll(e, 1, 0)) + (pltpu.roll(e, 127, 1) + pltpu.roll(e, 1, 1))
            e = ((1.0 - DAMPING) * e + f + (DAMPING / WEIGHT) * cr) * mask
        return e

    estimate = coarse(restrict(s_ref[PAD : PAD + WIDE, :]))
    corr_ref[PAD : PAD + WIDE, :] = prolong_rows(prolong_cols(estimate), spread_rows) * o_ref[PAD : PAD + WIDE, :]
    for i in chunks:
        c = corr_ref[pad_at(i), :]
        shift_ref[at(i), :] = o_ref[pad_at(i), :] * cross(corr_ref, i, c) - diag_ref[at(i), :] * c

    def goal(g, carry):
        sink = exits_ref.at[g]

        def next_d(old_ref, new_ref, i, a, b):
            mid, o = old_ref[pad_at(i), :], o_ref[pad_at(i), :]
            diag = diag_ref[at(i), :] + o * sink[at(i), :]
            r = r_ref[at(i), :] - diag * mid + o * cross(old_ref, i, mid)
            d = a * mid + b * r
            r_ref[at(i), :] = r
            new_ref[pad_at(i), :] = d
            x_ref[g, at(i), :] += d

        (a1, b1), (a2, b2), (a3, b3) = COEF
        for i in chunks:
            s, o = s_ref[pad_at(i), :], o_ref[pad_at(i), :]
            d = s * (1.0 / CENTER)
            r = r1_ref[at(i), :] - (o * sink[at(i), :]) * d
            n = a1 * d + b1 * r
            r_ref[at(i), :] = r
            da_ref[pad_at(i), :] = n
            x_ref[g, at(i), :] = d + n
        for i in chunks:
            next_d(da_ref, db_ref, i, a2, b2)
        for i in chunks:
            next_d(db_ref, da_ref, i, a3, b3)
        for i in chunks:
            mid, o = da_ref[pad_at(i), :], o_ref[pad_at(i), :]
            hit = o * sink[at(i), :]
            r = r_ref[at(i), :] - (diag_ref[at(i), :] + hit) * mid + o * cross(da_ref, i, mid)
            pool_ref[at(i), :] = r
            c = corr_ref[pad_at(i), :]
            r = r + shift_ref[at(i), :] - hit * c
            d = r * (1.0 / CENTER)
            r_ref[at(i), :] = r
            db_ref[pad_at(i), :] = d
            x_ref[g, at(i), :] += c + d
        grow_ref[g] = restrict(pool_ref[...])
        for i in chunks:
            next_d(db_ref, da_ref, i, a1, b1)
        for i in chunks:
            next_d(da_ref, db_ref, i, a2, b2)
        for i in range(HALO, HALO + ROWS, CHUNK):
            mid, o = db_ref[pad_at(i), :], o_ref[pad_at(i), :]
            diag = diag_ref[at(i), :] + o * sink[at(i), :]
            r = r_ref[at(i), :] - diag * mid + o * cross(db_ref, i, mid)
            x_ref[g, at(i), :] += a3 * mid + b3 * r
        return carry

    lax.fori_loop(0, GOALS, goal, 0)

    after = coarse(grow_ref[...].reshape(GOALS * CROWS, 128))
    wide = prolong_cols(after)
    o = o_ref[PAD + HALO : PAD + HALO + ROWS, 0:COLS]
    for g in range(GOALS):
        add = prolong_rows(wide[g * CROWS : (g + 1) * CROWS, 0:COLS], spread_rows[HALO : HALO + ROWS])
        out_ref[g] = x_ref[g, HALO : HALO + ROWS, 0:COLS] + o * add


def main(src, top, bottom, from_left, from_right, exits):
    padded = pltpu.VMEM((WIDE + 2 * PAD, LANES), F32)
    plain = pltpu.VMEM((WIDE, LANES), F32)
    return pl.pallas_call(
        main_kernel,
        out_shape=jax.ShapeDtypeStruct((GOALS, ROWS, COLS), F32),
        in_specs=[pl.BlockSpec(memory_space=pltpu.VMEM)] * 6,
        out_specs=pl.BlockSpec(memory_space=pltpu.VMEM),
        scratch_shapes=[
            padded, padded, plain, plain, padded, plain, padded, padded, plain,
            pltpu.VMEM((GOALS, WIDE, LANES), F32), plain, pltpu.VMEM((GOALS, CROWS, 128), F32),
        ],
        compiler_params=pltpu.CompilerParams(vmem_limit_bytes=32 * 2**20),
        cost_estimate=pl.CostEstimate(flops=10**8, bytes_accessed=2**20, transcendentals=0),
    )(src, top, bottom, from_left, from_right, exits)


def per_device(obstacles, load, exit_rows, exit_cols):
    gx, gy = lax.axis_index("gx"), lax.axis_index("gy")
    ny = lax.axis_size("gy")
    source = jnp.where(obstacles == 0, load, 0.0)
    first, last = source[:HALO], source[ROWS - HALO :]
    even = lax.rem(gx, 2) == 0
    nx = lax.axis_size("gx")
    inner = [(i, i ^ 1) for i in range(nx)]
    outer = [(i, j) for i in range(1, nx - 1) for j in [((i + 1) ^ 1) - 1]]
    got_outer = lax.ppermute(jnp.where(even, first, last), "gx", outer)
    got_inner = lax.ppermute(jnp.where(even, last, first), "gx", inner)
    exits = exits_of(exit_rows, exit_cols)
    top = jnp.where(even, got_outer, got_inner)
    bottom = jnp.where(even, got_inner, got_outer)
    left, right = pack(source, top, bottom)
    from_left = lax.ppermute(right, "gy", [(i, i + 1) for i in range(ny - 1)])
    from_right = lax.ppermute(left, "gy", [(i + 1, i) for i in range(ny - 1)])
    return main(source, top, bottom, from_left, from_right, exits)


def solution(mesh):
    in_specs = (P("gx", "gy"), P("gx", "gy"), P(), P())
    out_specs = P(None, "gx", "gy")
    return jax.shard_map(
        per_device, mesh=mesh, in_specs=in_specs, out_specs=out_specs, check_vma=False
    )
```

```python
import functools

import jax
import jax.numpy as jnp
import numpy as np
from jax import lax
from jax.experimental import pallas as pl
from jax.experimental.pallas import tpu as pltpu
from jax.sharding import PartitionSpec as P

SCREENING = 0.0001
EXIT_SINK = 4.0
WEIGHT = 4.01
DAMPING = 0.8
CENTER = 6.75
HALF = 5.75

GOALS = 4
ROWS = 128
COLS = 256
HALO = 16
WIDE = ROWS + 2 * HALO
LANES = 384
STEPS = WIDE // 8
CROWS = WIDE // 4
F32 = jnp.float32
BF16 = jnp.bfloat16

COEF = []
_q = CENTER / HALF
_p = 1.0 / _q
for _ in range(3):
    _n = 1.0 / (2.0 * _q - _p)
    COEF.append((_n * _p, 2.0 * _n / HALF))
    _p = _n


def split(x):
    high = x.astype(BF16)
    return high, (x - high.astype(F32)).astype(BF16)


def dot(a, b, dims=((1,), (0,))):
    return lax.dot_general(a, b, (dims, ((), ())), preferred_element_type=F32)


def iota(shape, dim):
    return lax.broadcasted_iota(jnp.int32, shape, dim)


def one_zero(condition):
    return jnp.where(condition, 1.0, 0.0).astype(F32)


def natural(p):
    return STEPS * (p & 7) + (p >> 3)


FAR = 1 << 20


def exits_kernel(rows_ref, cols_ref, out_ref):
    row0 = lax.axis_index("gx") * ROWS - HALO
    col0 = lax.axis_index("gy") * COLS
    count = rows_ref.shape[1] // 128

    keys = []
    for k in range(count):
        r = rows_ref[:, 128 * k : 128 * k + 128] - row0
        c = cols_ref[:, 128 * k : 128 * k + 128] - col0
        near = (r >= 0) & (r < WIDE) & (c >= -HALO) & (c < COLS + HALO)
        c = jnp.where(c < 0, c + COLS + HALO, jnp.where(c >= COLS, c + HALO, c))
        keys.append(jnp.where(near, r * 512 + c, FAR))

    def take(keys):
        least = functools.reduce(jnp.minimum, keys)
        return least, [jnp.where(k == least, FAR, k) for k in keys]

    row_at = natural(iota((WIDE, 256), 0))
    col_at = iota((COLS + 2 * HALO, 256), 0)

    def marks(g, one, two):
        key = jnp.concatenate([one[g : g + 1], two[g : g + 1]], axis=1)
        left = one_zero(row_at == (key >> 9)).astype(BF16)
        right = one_zero(col_at == (key & 511)).astype(BF16)
        return dot(left, right, ((1,), (1,)))

    def put(g, total):
        sink = jnp.minimum(total, 1.0) * EXIT_SINK
        out_ref[g, :, 0:COLS] = sink[:, :COLS]
        tail = jnp.concatenate([sink[:, COLS:], jnp.zeros((WIDE, 128 - 2 * HALO), F32)], axis=1)
        out_ref[g, :, COLS:LANES] = pltpu.roll(tail, 128 - HALO, 1)

    one, keys = take(keys)
    two, keys = take(keys)
    for g in range(GOALS):
        put(g, marks(g, one, two))

    def more(keys):
        return jnp.min(functools.reduce(jnp.minimum, keys)) < FAR

    def again(keys):
        one, keys = take(keys)
        two, keys = take(keys)
        for g in range(GOALS):
            extra = jnp.minimum(marks(g, one, two), 1.0) * EXIT_SINK
            out_ref[g, :, 0:COLS] = jnp.maximum(out_ref[g, :, 0:COLS], extra[:, :COLS])
            tail = jnp.concatenate([extra[:, COLS:], jnp.zeros((WIDE, 128 - 2 * HALO), F32)], axis=1)
            out_ref[g, :, COLS:LANES] = jnp.maximum(out_ref[g, :, COLS:LANES], pltpu.roll(tail, 128 - HALO, 1))
        return keys

    lax.while_loop(more, again, keys)


def exits_of(rows, cols):
    return pl.pallas_call(
        exits_kernel,
        out_shape=jax.ShapeDtypeStruct((GOALS, WIDE, LANES), F32),
        in_specs=[pl.BlockSpec(memory_space=pltpu.VMEM)] * 2,
        out_specs=pl.BlockSpec(memory_space=pltpu.VMEM),
        compiler_params=pltpu.CompilerParams(vmem_limit_bytes=8 * 2**20),
        cost_estimate=pl.CostEstimate(flops=2 * 4 * 256 * 160 * 288, bytes_accessed=2**20, transcendentals=0),
    )(rows, cols)


def pack_kernel(src_ref, outer_ref, inner_ref, left_ref, right_ref, top_ref, bottom_ref):
    even = lax.rem(lax.axis_index("gx"), 2) == 0
    top_ref[...] = jnp.where(even, outer_ref[...], inner_ref[...])
    bottom_ref[...] = jnp.where(even, inner_ref[...], outer_ref[...])

    def tile(q, lo):
        if q < HALO // 8:
            return top_ref[8 * q : 8 * q + 8, lo : lo + 128]
        if q >= (HALO + ROWS) // 8:
            at = 8 * q - HALO - ROWS
            return bottom_ref[at : at + 8, lo : lo + 128]
        at = 8 * q - HALO
        return src_ref[at : at + 8, lo : lo + 128]

    lane = iota((8, 128), 1)
    for b in range(LANES // 128):
        left = jnp.zeros((8, 128), F32)
        right = jnp.zeros((8, 128), F32)
        for m in range(8):
            q = 8 * b + m
            if q >= WIDE // 8:
                break
            here = (lane >= HALO * m) & (lane < HALO * (m + 1))
            left = jnp.where(here, pltpu.roll(tile(q, 0), HALO * m, 1), left)
            right = jnp.where(here, pltpu.roll(tile(q, COLS - 128), (HALO * m + HALO) % 128, 1), right)
        left_ref[:, 128 * b : 128 * b + 128] = left
        right_ref[:, 128 * b : 128 * b + 128] = right


def pack(src, outer, inner):
    return pl.pallas_call(
        pack_kernel,
        out_shape=[jax.ShapeDtypeStruct((8, LANES), F32)] * 2 + [jax.ShapeDtypeStruct((HALO, COLS), F32)] * 2,
        in_specs=[pl.BlockSpec(memory_space=pltpu.VMEM)] * 3,
        out_specs=[pl.BlockSpec(memory_space=pltpu.VMEM)] * 4,
        compiler_params=pltpu.CompilerParams(vmem_limit_bytes=4 * 2**20),
    )(src, outer, inner)


def main_kernel(
    src_ref, top_ref, bottom_ref, from_left_ref, from_right_ref, exits_ref, out_ref,
    nat_ref, s_ref, o_ref, diag_ref, r1_ref, corr_ref, shift_ref, dg_ref, da_ref, db_ref, r_ref, x_ref, y_ref, pool_ref, grow_ref,
):
    gx, gy = lax.axis_index("gx"), lax.axis_index("gy")

    for b in range(COLS // 128):
        at = slice(128 * b, 128 * b + 128)
        nat_ref[b, 0:HALO, :] = top_ref[:, at]
        nat_ref[b, HALO : HALO + ROWS, :] = src_ref[:, at]
        nat_ref[b, HALO + ROWS : WIDE, :] = bottom_ref[:, at]
    lane = iota((8, 128), 1)
    for q in range(STEPS):
        b, m = divmod(q, 8)
        at = slice(128 * b, 128 * b + 128)
        ahead = pltpu.roll(from_right_ref[:, at], (128 - HALO * m) % 128, 1)
        behind = pltpu.roll(from_left_ref[:, at], (128 - HALO - HALO * m) % 128, 1)
        both = jnp.where(lane < HALO, ahead, jnp.where(lane >= 128 - HALO, behind, 0.0))
        nat_ref[COLS // 128, 8 * q : 8 * q + 8, :] = both

    def ends(ref, first, last):
        ref[0] = pltpu.roll(last, 1, 0)
        ref[STEPS + 1] = pltpu.roll(first, 7, 0)

    def sweep(ref, body):
        before, mid = ref[0], ref[1]
        results = []
        for t in range(STEPS):
            after = ref[t + 2]
            beside = pltpu.roll(mid, LANES - 1, 1) + pltpu.roll(mid, 1, 1)
            results.append(body(t, mid, (after + before) + beside))
            before, mid = mid, after
        return results[0], results[-1]

    for t in range(STEPS):
        s = jnp.concatenate([nat_ref[b, pl.ds(t, 8, stride=STEPS), :] for b in range(LANES // 128)], axis=1)
        o = one_zero(s > 0.0)
        s_ref[t + 1] = s
        o_ref[t + 1] = o
    ends(s_ref, s_ref[1], s_ref[STEPS])
    ends(o_ref, o_ref[1], o_ref[STEPS])

    def first_diag(t, o, cross):
        diag_ref[t] = SCREENING + 4.0 * (1.0 - o) + o * cross

    sweep(o_ref, first_diag)

    def first_r(t, s, cross):
        r1_ref[t] = s - diag_ref[t] * (s * (1.0 / CENTER)) + o_ref[t + 1] * (cross * (1.0 / CENTER))

    sweep(s_ref, first_r)

    fine_col, coarse_col = iota((LANES, 128), 0), iota((LANES, 128), 1)
    fine_col = jnp.where(fine_col >= 320, fine_col - LANES, fine_col)
    coarse_col = jnp.where(coarse_col >= 96, coarse_col - 128, coarse_col)
    gather_cols = jnp.where((fine_col >> 2) == coarse_col, 0.25, 0.0).astype(BF16)
    fine_row, coarse_row = natural(iota((CROWS, WIDE), 1)), iota((CROWS, WIDE), 0)
    gather_rows = jnp.where((fine_row >> 2) == coarse_row, 0.25, 0.0).astype(BF16)
    gather_rows = jnp.concatenate([gather_rows, gather_rows], axis=1)
    spread_c, spread_f = iota((256, LANES), 0) & 127, iota((256, LANES), 1)
    spread_c = jnp.where(spread_c >= 96, spread_c - 128, spread_c)
    spread_f = jnp.where(spread_f >= 320, spread_f - LANES, spread_f)
    spread_cols = one_zero(spread_c == (spread_f >> 2)).astype(BF16)

    def spread_of(fine):
        c = iota(fine.shape, 1)
        c = jnp.where(c >= CROWS, c - CROWS, c)
        return one_zero((fine >> 2) == c).astype(BF16)

    def restrict(field):
        high, low = split(field)
        part = dot(high, gather_cols) + dot(low, gather_cols)
        high, low = split(part)
        return dot(gather_rows, jnp.concatenate([high, low], axis=0))

    def prolong_cols(e):
        high, low = split(e)
        return dot(jnp.concatenate([high, low], axis=1), spread_cols)

    def prolong_rows(e, spread):
        high, low = split(e)
        return dot(spread, jnp.concatenate([high, low], axis=0))

    def coarse(f):
        n = f.shape[0]
        row = gx * (ROWS // 4) + (lax.rem(iota((n, 128), 0), CROWS) - HALO // 4)
        col = iota((n, 128), 1)
        col = gy * (COLS // 4) + jnp.where(col >= 96, col - 128, col)
        inside = (row >= 0) & (row < 32 * (ROWS // 4)) & (col >= 0) & (col < 16 * (COLS // 4))
        mask = one_zero(inside)
        f = f * (DAMPING / WEIGHT)
        e = f * mask
        for _ in range(3):
            cr = (pltpu.roll(e, n - 1, 0) + pltpu.roll(e, 1, 0)) + (pltpu.roll(e, 127, 1) + pltpu.roll(e, 1, 1))
            e = ((1.0 - DAMPING) * e + f + (DAMPING / WEIGHT) * cr) * mask
        return e

    estimate = coarse(restrict(s_ref[1 : STEPS + 1].reshape(WIDE, LANES)))
    wide = prolong_rows(prolong_cols(estimate), spread_of(natural(iota((WIDE, 2 * CROWS), 0))))
    for t in range(STEPS):
        corr_ref[t + 1] = wide[8 * t : 8 * t + 8] * o_ref[t + 1]
    ends(corr_ref, corr_ref[1], corr_ref[STEPS])

    def first_shift(t, c, cross):
        shift_ref[t] = o_ref[t + 1] * cross - diag_ref[t] * c

    sweep(corr_ref, first_shift)

    (a1, b1), (a2, b2), (a3, b3) = COEF

    def goal(g, carry):
        def advance(old_ref, new_ref, a, b, also=None):
            def body(t, mid, cross):
                r = r_ref[t] - dg_ref[t] * mid + o_ref[t + 1] * cross
                d = a * mid + b * r
                r_ref[t] = r
                new_ref[t + 1] = d
                if also is not None:
                    also(t, mid, d)
                return d

            ends(new_ref, *sweep(old_ref, body))

        new = []
        for t in range(STEPS):
            s = s_ref[t + 1]
            hit = o_ref[t + 1] * exits_ref[g, 8 * t : 8 * t + 8, :]
            d = s * (1.0 / CENTER)
            r = r1_ref[t] - hit * d
            n = a1 * d + b1 * r
            dg_ref[t] = diag_ref[t] + hit
            r_ref[t] = r
            da_ref[t + 1] = n
            new.append(n)
        ends(da_ref, new[0], new[-1])

        def sum_1(t, mid, d):
            x_ref[g, t] = s_ref[t + 1, :, 0:COLS] * (1.0 / CENTER) + mid[:, :COLS] + d[:, :COLS]

        advance(da_ref, db_ref, a2, b2, sum_1)
        advance(db_ref, da_ref, a3, b3)

        def middle(t, mid, cross):
            o, c = o_ref[t + 1], corr_ref[t + 1]
            dg = dg_ref[t]
            r = r_ref[t] - dg * mid + o * cross
            pool_ref[t] = r
            r = r + shift_ref[t] - (dg - diag_ref[t]) * c
            d = r * (1.0 / CENTER)
            r_ref[t] = r
            db_ref[t + 1] = d
            x_ref[g, t] += (mid + c + d)[:, :COLS]
            return d

        ends(db_ref, *sweep(da_ref, middle))
        grow_ref[g] = restrict(pool_ref[...].reshape(WIDE, LANES))
        advance(db_ref, da_ref, a1, b1)

        def sum_2(t, mid, d):
            x_ref[g, t] += mid[:, :COLS] + d[:, :COLS]

        advance(da_ref, db_ref, a2, b2, sum_2)

        def last(t, mid, cross):
            r = r_ref[t] - dg_ref[t] * mid + o_ref[t + 1] * cross
            y = x_ref[g, t] + (a3 * mid + b3 * r)[:, :COLS]
            for b in range(COLS // 128):
                y_ref[g, b, pl.ds(t, 8, stride=STEPS), :] = y[:, 128 * b : 128 * b + 128]

        sweep(db_ref, last)
        return carry

    lax.fori_loop(0, GOALS, goal, 0)

    after = coarse(grow_ref[...].reshape(GOALS * CROWS, 128))
    wide = prolong_cols(after)
    spread = spread_of(iota((ROWS, 2 * CROWS), 0) + HALO)
    o = one_zero(src_ref[...] > 0.0)
    for g in range(GOALS):
        add = prolong_rows(wide[g * CROWS : (g + 1) * CROWS, 0:COLS], spread)
        add = o * add
        for b in range(COLS // 128):
            at = slice(128 * b, 128 * b + 128)
            out_ref[g, :, at] = y_ref[g, b, HALO : HALO + ROWS, :] + add[:, at]


def main(src, top, bottom, from_left, from_right, exits):
    padded = pltpu.VMEM((STEPS + 2, 8, LANES), F32)
    plain = pltpu.VMEM((STEPS, 8, LANES), F32)
    return pl.pallas_call(
        main_kernel,
        out_shape=jax.ShapeDtypeStruct((GOALS, ROWS, COLS), F32),
        in_specs=[pl.BlockSpec(memory_space=pltpu.VMEM)] * 6,
        out_specs=pl.BlockSpec(memory_space=pltpu.VMEM),
        scratch_shapes=[
            pltpu.VMEM((LANES // 128, WIDE, 128), F32), padded, padded, plain, plain, padded, plain, plain, padded, padded, plain,
            pltpu.VMEM((GOALS, STEPS, 8, COLS), F32), pltpu.VMEM((GOALS, COLS // 128, WIDE, 128), F32), plain,
            pltpu.VMEM((GOALS, CROWS, 128), F32),
        ],
        compiler_params=pltpu.CompilerParams(vmem_limit_bytes=16 * 2**20),
        cost_estimate=pl.CostEstimate(flops=10**8, bytes_accessed=2**20, transcendentals=0),
    )(src, top, bottom, from_left, from_right, exits)


def per_device(obstacles, load, exit_rows, exit_cols):
    gx, gy = lax.axis_index("gx"), lax.axis_index("gy")
    ny = lax.axis_size("gy")
    source = jnp.where(obstacles == 0, load, 0.0)
    first, last = source[:HALO], source[ROWS - HALO :]
    even = lax.rem(gx, 2) == 0
    nx = lax.axis_size("gx")
    inner = [(i, i ^ 1) for i in range(nx)]
    outer = [(i, j) for i in range(1, nx - 1) for j in [((i + 1) ^ 1) - 1]]
    got_outer = lax.ppermute(jnp.where(even, first, last), "gx", outer)
    got_inner = lax.ppermute(jnp.where(even, last, first), "gx", inner)
    exits = exits_of(exit_rows, exit_cols)
    left, right, top, bottom = pack(source, got_outer, got_inner)
    from_left = lax.ppermute(right, "gy", [(i, i + 1) for i in range(ny - 1)])
    from_right = lax.ppermute(left, "gy", [(i + 1, i) for i in range(ny - 1)])
    return main(source, top, bottom, from_left, from_right, exits)


def solution(mesh):
    in_specs = (P("gx", "gy"), P("gx", "gy"), P(), P())
    out_specs = P(None, "gx", "gy")
    return jax.shard_map(
        per_device, mesh=mesh, in_specs=in_specs, out_specs=out_specs, check_vma=False
    )
```

```python
import functools

import jax
import jax.numpy as jnp
import numpy as np
from jax import lax
from jax.experimental import pallas as pl
from jax.experimental.pallas import tpu as pltpu
from jax.sharding import PartitionSpec as P

SCREENING = 0.0001
EXIT_SINK = 4.0
WEIGHT = 4.01
DAMPING = 0.8
CENTER = 6.75
HALF = 5.75

GOALS = 4
ROWS = 128
COLS = 256
HALO = 16
WIDE = ROWS + 2 * HALO
STRIP = WIDE * HALO // 8 + 64
FRINGE = 128
KEPT = FRINGE // 2 - HALO
STEPS = WIDE // 8
CROWS = WIDE // 4
F32 = jnp.float32
BF16 = jnp.bfloat16

COEF = []
_q = CENTER / HALF
_p = 1.0 / _q
for _ in range(3):
    _n = 1.0 / (2.0 * _q - _p)
    COEF.append((_n * _p, 2.0 * _n / HALF))
    _p = _n


def split(x):
    high = x.astype(BF16)
    return high, (x - high.astype(F32)).astype(BF16)


def dot(a, b, dims=((1,), (0,))):
    return lax.dot_general(a, b, (dims, ((), ())), preferred_element_type=F32)


def iota(shape, dim):
    return lax.broadcasted_iota(jnp.int32, shape, dim)


def one_zero(condition):
    return jnp.where(condition, 1.0, 0.0).astype(F32)


def natural(p):
    return STEPS * (p & 7) + (p >> 3)


FAR = 1 << 20


def mark_exits(rows_ref, cols_ref, inner_ref, fringe_ref):
    row0 = lax.axis_index("gx") * ROWS - HALO
    col0 = lax.axis_index("gy") * COLS - HALO
    keys = []
    for k in range(rows_ref.shape[1] // 128):
        r = rows_ref[:, 128 * k : 128 * k + 128] - row0
        c = cols_ref[:, 128 * k : 128 * k + 128] - col0
        near = (r >= 0) & (r < WIDE) & (c >= 0) & (c < COLS + 2 * HALO)
        keys.append(jnp.where(near, r * 512 + c, FAR))

    def take(keys):
        least = functools.reduce(jnp.minimum, keys)
        return least, [jnp.where(k == least, FAR, k) for k in keys]

    row_at = natural(iota((WIDE, 256), 0))
    inner_at = iota((COLS, 256), 0) + HALO
    fringe_at = iota((FRINGE, 256), 0)
    fringe_at = jnp.where(fringe_at < FRINGE // 2, fringe_at, fringe_at + (COLS + 2 * HALO - FRINGE))

    def marks(g, one, two):
        key = jnp.concatenate([one[g : g + 1], two[g : g + 1]], axis=1)
        at_row = one_zero(row_at == (key >> 9)).astype(BF16)
        col = key & 511
        for ref, at in ((inner_ref, inner_at), (fringe_ref, fringe_at)):
            count = dot(at_row, one_zero(at == col).astype(BF16), ((1,), (1,)))
            yield ref, jnp.minimum(count, 1.0) * EXIT_SINK

    one, keys = take(keys)
    two, keys = take(keys)
    for g in range(GOALS):
        for ref, sink in marks(g, one, two):
            ref[g] = sink

    def more(keys):
        return jnp.min(functools.reduce(jnp.minimum, keys)) < FAR

    def again(keys):
        one, keys = take(keys)
        two, keys = take(keys)
        for g in range(GOALS):
            for ref, sink in marks(g, one, two):
                ref[g] = jnp.maximum(ref[g], sink)
        return keys

    lax.while_loop(more, again, keys)


def run_cycles(width, column, nat_ref, exits_ref, scratch, finish):
    s_ref, o_ref, diag_ref, r1_ref, corr_ref, shift_ref, dg_ref, da_ref, db_ref, r_ref, x_ref, y_ref, pool_ref, grow_ref = scratch
    gx, gy = lax.axis_index("gx"), lax.axis_index("gy")
    tiles = range(width // 128)

    def ends(ref, first, last):
        ref[0] = pltpu.roll(last, 1, 0)
        ref[STEPS + 1] = pltpu.roll(first, 7, 0)

    def sweep(ref, body):
        before, mid = ref[0], ref[1]
        results = []
        for t in range(STEPS):
            after = ref[t + 2]
            beside = pltpu.roll(mid, width - 1, 1) + pltpu.roll(mid, 1, 1)
            results.append(body(t, mid, (after + before) + beside))
            before, mid = mid, after
        return results[0], results[-1]

    for t in range(STEPS):
        s = jnp.concatenate([nat_ref[b, pl.ds(t, 8, stride=STEPS), :] for b in tiles], axis=1)
        s_ref[t + 1] = s
        o_ref[t + 1] = one_zero(s > 0.0)
    ends(s_ref, s_ref[1], s_ref[STEPS])
    ends(o_ref, o_ref[1], o_ref[STEPS])

    def first_diag(t, o, cross):
        diag_ref[t] = SCREENING + 4.0 * (1.0 - o) + o * cross

    sweep(o_ref, first_diag)

    def first_r(t, s, cross):
        r1_ref[t] = s - diag_ref[t] * (s * (1.0 / CENTER)) + o_ref[t + 1] * (cross * (1.0 / CENTER))

    sweep(s_ref, first_r)

    gather_cols = jnp.where((iota((width, 128), 0) >> 2) == iota((width, 128), 1), 0.25, 0.0).astype(BF16)
    gather_rows = jnp.where((natural(iota((CROWS, WIDE), 1)) >> 2) == iota((CROWS, WIDE), 0), 0.25, 0.0).astype(BF16)
    gather_rows = jnp.concatenate([gather_rows, gather_rows], axis=1)
    spread_cols = one_zero((iota((256, width), 0) & 127) == (iota((256, width), 1) >> 2)).astype(BF16)

    def spread_of(fine):
        c = iota(fine.shape, 1)
        c = jnp.where(c >= CROWS, c - CROWS, c)
        return one_zero((fine >> 2) == c).astype(BF16)

    def restrict(field):
        high, low = split(field)
        part = dot(high, gather_cols) + dot(low, gather_cols)
        high, low = split(part)
        return dot(gather_rows, jnp.concatenate([high, low], axis=0))

    def prolong_cols(e):
        high, low = split(e)
        return dot(jnp.concatenate([high, low], axis=1), spread_cols)

    def prolong_rows(e, spread):
        high, low = split(e)
        return dot(spread, jnp.concatenate([high, low], axis=0))

    def coarse(f):
        n = f.shape[0]
        row = gx * (ROWS // 4) + (lax.rem(iota((n, 128), 0), CROWS) - HALO // 4)
        lane = iota((n, 128), 1)
        col = gy * (COLS // 4) + column(lane)
        inside = (row >= 0) & (row < 32 * (ROWS // 4)) & (col >= 0) & (col < 16 * (COLS // 4)) & (lane < width // 4)
        mask = one_zero(inside)
        f = f * (DAMPING / WEIGHT)
        e = f * mask
        for _ in range(3):
            cr = (pltpu.roll(e, n - 1, 0) + pltpu.roll(e, 1, 0)) + (pltpu.roll(e, 127, 1) + pltpu.roll(e, 1, 1))
            e = ((1.0 - DAMPING) * e + f + (DAMPING / WEIGHT) * cr) * mask
        return e

    estimate = coarse(restrict(s_ref[1 : STEPS + 1].reshape(WIDE, width)))
    wide = prolong_rows(prolong_cols(estimate), spread_of(natural(iota((WIDE, 2 * CROWS), 0))))
    for t in range(STEPS):
        corr_ref[t + 1] = wide[8 * t : 8 * t + 8] * o_ref[t + 1]
    ends(corr_ref, corr_ref[1], corr_ref[STEPS])

    def first_shift(t, c, cross):
        shift_ref[t] = o_ref[t + 1] * cross - diag_ref[t] * c

    sweep(corr_ref, first_shift)

    (a1, b1), (a2, b2), (a3, b3) = COEF

    for g in range(GOALS):

        def advance(old_ref, new_ref, a, b, also=None):
            def body(t, mid, cross):
                r = r_ref[t] - dg_ref[t] * mid + o_ref[t + 1] * cross
                d = a * mid + b * r
                r_ref[t] = r
                new_ref[t + 1] = d
                if also is not None:
                    also(t, mid, d)
                return d

            ends(new_ref, *sweep(old_ref, body))

        new = []
        for t in range(STEPS):
            hit = o_ref[t + 1] * exits_ref[g, 8 * t : 8 * t + 8, :]
            d = s_ref[t + 1] * (1.0 / CENTER)
            r = r1_ref[t] - hit * d
            n = a1 * d + b1 * r
            dg_ref[t] = diag_ref[t] + hit
            r_ref[t] = r
            da_ref[t + 1] = n
            new.append(n)
        ends(da_ref, new[0], new[-1])

        def sum_1(t, mid, d):
            x_ref[t] = s_ref[t + 1] * (1.0 / CENTER) + mid + d

        advance(da_ref, db_ref, a2, b2, sum_1)
        advance(db_ref, da_ref, a3, b3)

        def middle(t, mid, cross):
            o, c = o_ref[t + 1], corr_ref[t + 1]
            dg = dg_ref[t]
            r = r_ref[t] - dg * mid + o * cross
            pool_ref[t] = r
            r = r + shift_ref[t] - (dg - diag_ref[t]) * c
            d = r * (1.0 / CENTER)
            r_ref[t] = r
            db_ref[t + 1] = d
            x_ref[t] += mid + c + d
            return d

        ends(db_ref, *sweep(da_ref, middle))
        grow_ref[g] = restrict(pool_ref[...].reshape(WIDE, width))
        advance(db_ref, da_ref, a1, b1)

        def sum_2(t, mid, d):
            x_ref[t] += mid + d

        advance(da_ref, db_ref, a2, b2, sum_2)

        def last(t, mid, cross):
            r = r_ref[t] - dg_ref[t] * mid + o_ref[t + 1] * cross
            y = x_ref[t] + (a3 * mid + b3 * r)
            for b in tiles:
                y_ref[g, b, pl.ds(t, 8, stride=STEPS), :] = y[:, 128 * b : 128 * b + 128]

        sweep(db_ref, last)

    after = coarse(grow_ref[...].reshape(GOALS * CROWS, 128))
    wide = prolong_cols(after)
    spread = spread_of(iota((ROWS, 2 * CROWS), 0) + HALO)
    for g in range(GOALS):
        add = prolong_rows(wide[g * CROWS : (g + 1) * CROWS], spread)
        for b in tiles:
            o = one_zero(nat_ref[b, HALO : HALO + ROWS, :] > 0.0)
            finish(g, b, y_ref[g, b, HALO : HALO + ROWS, :] + o * add[:, 128 * b : 128 * b + 128])


def scratch_of(width):
    padded = pltpu.VMEM((STEPS + 2, 8, width), F32)
    plain = pltpu.VMEM((STEPS, 8, width), F32)
    return [
        pltpu.VMEM((width // 128, WIDE, 128), F32), padded, padded, plain, plain, padded, plain, plain, padded, padded, plain,
        plain, pltpu.VMEM((GOALS, width // 128, WIDE, 128), F32), plain, pltpu.VMEM((GOALS, CROWS, 128), F32),
    ]


def starts_early():
    return lax.axis_index("gy") == 8


def tile_of(src_ref, top_ref, bottom_ref, q, lo):
    if q < HALO // 8:
        return top_ref[8 * q : 8 * q + 8, lo : lo + 128]
    if q >= (HALO + ROWS) // 8:
        at = 8 * q - HALO - ROWS
        return bottom_ref[at : at + 8, lo : lo + 128]
    at = 8 * q - HALO
    return src_ref[at : at + 8, lo : lo + 128]


def do_tile(src_ref, top_ref, bottom_ref, rows_ref, cols_ref, part_ref, fringe_exits_ref, exits_ref, nat_ref, scratch):
    mark_exits(rows_ref, cols_ref, exits_ref, fringe_exits_ref)
    for b in range(COLS // 128):
        at = slice(128 * b, 128 * b + 128)
        nat_ref[b, 0:HALO, :] = top_ref[:, at]
        nat_ref[b, HALO : HALO + ROWS, :] = src_ref[:, at]
        nat_ref[b, HALO + ROWS : WIDE, :] = bottom_ref[:, at]

    def finish(g, b, x):
        part_ref[g, :, 128 * b : 128 * b + 128] = x

    run_cycles(COLS, lambda lane: lane, nat_ref, exits_ref, scratch, finish)


def early_kernel(
    src_ref, inner_ref, outer_ref, rows_ref, cols_ref,
    left_ref, right_ref, top_ref, bottom_ref, part_ref, fringe_exits_ref, exits_ref, nat_ref, *scratch,
):
    even = lax.rem(lax.axis_index("gx"), 2) == 0
    top_ref[...] = jnp.where(even, outer_ref[...], inner_ref[...])
    bottom_ref[...] = jnp.where(even, inner_ref[...], outer_ref[...])

    lane = iota((8, 128), 1)
    for b in range(STRIP // 128):
        left = jnp.zeros((8, 128), F32)
        right = jnp.zeros((8, 128), F32)
        for m in range(8):
            q = 8 * b + m
            if q >= STEPS:
                break
            here = (lane >= HALO * m) & (lane < HALO * (m + 1))
            first = tile_of(src_ref, top_ref, bottom_ref, q, 0)
            last = tile_of(src_ref, top_ref, bottom_ref, q, COLS - 128)
            left = jnp.where(here, pltpu.roll(first, HALO * m, 1), left)
            right = jnp.where(here, pltpu.roll(last, (HALO * m + HALO) % 128, 1), right)
        left_ref[:, 128 * b : 128 * b + 128] = left
        right_ref[:, 128 * b : 128 * b + 128] = right

    @pl.when(starts_early())
    def _():
        do_tile(src_ref, top_ref, bottom_ref, rows_ref, cols_ref, part_ref, fringe_exits_ref, exits_ref, nat_ref, scratch)


def late_kernel(
    src_ref, top_ref, bottom_ref, rows_ref, cols_ref, part_ref, fringe_exits_ref, exits_ref, nat_ref, *scratch
):
    @pl.when(jnp.logical_not(starts_early()))
    def _():
        do_tile(src_ref, top_ref, bottom_ref, rows_ref, cols_ref, part_ref, fringe_exits_ref, exits_ref, nat_ref, scratch)


STRIPS = [jax.ShapeDtypeStruct((8, STRIP), F32)] * 2 + [jax.ShapeDtypeStruct((HALO, COLS), F32)] * 2
PARTS = [jax.ShapeDtypeStruct((GOALS, ROWS, COLS), F32), jax.ShapeDtypeStruct((GOALS, WIDE, FRINGE), F32)]


def whole(count):
    return [pl.BlockSpec(memory_space=pltpu.VMEM)] * count


def call(kernel, outs, width, *args):
    exits = [pltpu.VMEM((GOALS, WIDE, width), F32)]
    return pl.pallas_call(
        kernel,
        out_shape=outs,
        in_specs=whole(len(args)),
        out_specs=whole(len(outs)),
        scratch_shapes=exits + scratch_of(width),
        compiler_params=pltpu.CompilerParams(vmem_limit_bytes=16 * 2**20),
        cost_estimate=pl.CostEstimate(flops=10**7, bytes_accessed=2**20, transcendentals=0),
    )(*args)


def fringe_kernel(
    src_ref, top_ref, bottom_ref, from_left_ref, from_right_ref, part_a_ref, exits_a_ref, part_b_ref, exits_b_ref, out_ref,
    exits_ref, nat_ref, *scratch,
):
    early = starts_early()
    lane = iota((8, 128), 1)
    half = FRINGE // 2
    for q in range(STEPS):
        b, m = divmod(q, 8)
        at = slice(128 * b, 128 * b + 128)
        behind = pltpu.roll(from_left_ref[:, at], (128 - HALO * m) % 128, 1)
        ahead = pltpu.roll(from_right_ref[:, at], (128 - HALO - HALO * m) % 128, 1)
        first = pltpu.roll(tile_of(src_ref, top_ref, bottom_ref, q, 0), HALO, 1)
        last = pltpu.roll(tile_of(src_ref, top_ref, bottom_ref, q, COLS - 128), 128 - HALO, 1)
        right = jnp.where(lane < 128 - HALO, last, ahead)
        nat_ref[0, 8 * q : 8 * q + 8, :] = jnp.where(lane < HALO, behind, jnp.where(lane < half, first, right))

    exits_ref[...] = jnp.where(early, exits_a_ref[...], exits_b_ref[...])
    lanes = iota((ROWS, 128), 1)

    def column(lane):
        return jnp.where(lane < half // 4, lane - HALO // 4, lane + (COLS + HALO - FRINGE) // 4)

    def finish(g, b, x):
        first = pltpu.roll(x, 128 - HALO, 1)
        last = pltpu.roll(x, HALO, 1)
        part = jnp.where(early, part_a_ref[g], part_b_ref[g])
        out_ref[g, :, 0:128] = jnp.where(lanes < HALO, first, part[:, 0:128])
        out_ref[g, :, 128:256] = jnp.where(lanes >= 128 - HALO, last, part[:, 128:256])

    run_cycles(FRINGE, column, nat_ref, exits_ref, scratch, finish)


def per_device(obstacles, load, exit_rows, exit_cols):
    gx = lax.axis_index("gx")
    nx, ny = lax.axis_size("gx"), lax.axis_size("gy")
    even = lax.rem(gx, 2) == 0
    source = jnp.where(obstacles == 0, load, 0.0)
    first, last = source[:HALO], source[ROWS - HALO :]
    got_inner = lax.ppermute(jnp.where(even, last, first), "gx", [(i, i ^ 1) for i in range(nx)])
    outer = [(i, ((i + 1) ^ 1) - 1) for i in range(1, nx - 1)]
    got_outer = lax.ppermute(jnp.where(even, first, last), "gx", outer)
    left, right, top, bottom, part_a, exits_a = call(
        early_kernel, STRIPS + PARTS, COLS, source, got_inner, got_outer, exit_rows, exit_cols
    )
    from_left = lax.ppermute(right, "gy", [(i, i + 1) for i in range(ny - 1)])
    from_right = lax.ppermute(left, "gy", [(i + 1, i) for i in range(ny - 1)])
    part_b, exits_b = call(late_kernel, PARTS, COLS, source, top, bottom, exit_rows, exit_cols)
    (out,) = call(
        fringe_kernel, PARTS[:1], FRINGE,
        source, top, bottom, from_left, from_right, part_a, exits_a, part_b, exits_b,
    )
    return out


def solution(mesh):
    in_specs = (P("gx", "gy"), P("gx", "gy"), P(), P())
    out_specs = P(None, "gx", "gy")
    return jax.shard_map(
        per_device, mesh=mesh, in_specs=in_specs, out_specs=out_specs, check_vma=False
    )
```
